512 devices in a mesh: row: 16 (over x, z_hi, core), col: 32 (over z_lo, y).
Axes of the slice: x: 4, y: 4, z: 16 (z_hi: 2, z_lo: 8; z = z_hi * 8 + z_lo), core: 2. Of those that a mesh axis runs over, the one named last changes fastest.
Arguments:
- output_gradient: bfloat16 [512, 16384], P('col', 'row'), may hold values from -6 to 6
- codes: bfloat16 [53248, 16384], P('col', 'row'), may hold values from -4 to 4
- feature_scale: float32 [16384], P('row'), may hold values from 0.002 to 0.02
- adapter_down_map: bfloat16 [16, 53248], P(None, 'col'), may hold values from -1.5 to 1.5
- adapter_up_map: bfloat16 [16, 16384], P(None, 'row'), may hold values from -0.046875 to 0.046875
- stored_activation: bfloat16 [512, 53248], P('row', 'col'), may hold values from -1 to 1
Outputs:
- activation_derivative: bfloat16 [512, 53248], P('row', 'col')
- compress_matrix_derivative: float32 [16, 53248], P(None, ('col', 'row'))
The draws below stay inside these ranges and needn't reach their ends.
All inputs are finite; a program needn't handle non-finite values.
Results may differ from the reference program's by a relative error of at most 0.0049.
Values may be sent and summed in bfloat16 or wider, within the bound.
A program may use at most 64 MiB of HBM per device.

```python
import math
import jax
import jax.numpy as jnp
from jax import lax

MODEL_WIDTH = 16384
HIDDEN_UNITS = 53248
ADAPTER_RANK = 16
TOKENS = 512


def level_of(key, extent, pieces, least, high):
    factor_of = 1.0
    for position, shards_of in pieces:
        heights = jax.random.uniform(jax.random.fold_in(jax.random.fold_in(key, 6), position), (shards_of,), jnp.float32, least / len(pieces), high / len(pieces))
        factor_of = factor_of * jnp.repeat(jnp.exp(heights), extent[position] // shards_of).reshape((-1,) + (1,) * (len(extent) - 1 - position))
    return factor_of


def noise(rng, shape, spread, most, shards=(), kind=jnp.bfloat16):
    array = spread * jax.random.normal(rng, shape, jnp.float32)
    if shards:
        array = array * level_of(rng, shape, shards, -0.22, 0.18)
    return jnp.clip(array, -most, most).astype(kind)


def setup_inputs(seed: int = 0) -> dict:
    arg_keys = jax.random.split(jax.random.key(seed), 7)
    output_gradient = noise(arg_keys[0], (TOKENS, MODEL_WIDTH), 1.0, 6.0, ((0, 32), (1, 16)))
    codes = noise(arg_keys[1], (HIDDEN_UNITS, MODEL_WIDTH), 1.0, 4.0, ((0, 32), (1, 16)))
    feature_scale = jnp.clip(jnp.exp(math.log(0.02) - 2.30258502 * jax.random.uniform(arg_keys[2], (MODEL_WIDTH,), jnp.float32) ** level_of(arg_keys[2], (MODEL_WIDTH,), ((0, 16),), -0.2, 0.2)), 0.002, 0.02)
    adapter_down_map = noise(arg_keys[3], (ADAPTER_RANK, HIDDEN_UNITS), ADAPTER_RANK ** -0.5, 1.5, ((1, 32),))
    adapter_up_map = noise(arg_keys[4], (ADAPTER_RANK, MODEL_WIDTH), MODEL_WIDTH ** -0.5, 0.046875, ((1, 16),))
    stored_activation = noise(arg_keys[5], (TOKENS, HIDDEN_UNITS), 0.1, 1.0, ((0, 16), (1, 32)))
    return dict(output_gradient=output_gradient, codes=codes, feature_scale=feature_scale, adapter_down_map=adapter_down_map, adapter_up_map=adapter_up_map, stored_activation=stored_activation)


correction_multiplier = 0.5


def reference(output_gradient, codes, feature_scale, adapter_down_map, adapter_up_map, stored_activation):
    scaled = (output_gradient.astype(jnp.float32) * feature_scale[None, :]).astype(jnp.bfloat16)
    bottleneck_derivative = lax.dot_general(output_gradient, adapter_up_map, (((1,), (1,)), ((), ())), preferred_element_type=jnp.float32)
    bottleneck_derivative_narrowed = bottleneck_derivative.astype(jnp.bfloat16)
    main_branch = lax.dot_general(scaled, codes, (((1,), (1,)), ((), ())), preferred_element_type=jnp.float32)
    adapter_term = jnp.dot(bottleneck_derivative_narrowed, adapter_down_map, preferred_element_type=jnp.float32)
    activation_derivative = (main_branch + correction_multiplier * adapter_term).astype(jnp.bfloat16)
    compress_matrix_derivative = correction_multiplier * lax.dot_general(bottleneck_derivative_narrowed, stored_activation, (((0,), (0,)), ((), ())), preferred_element_type=jnp.float32)
    return activation_derivative, compress_matrix_derivative
```

```python
import jax
import jax.numpy as jnp
from jax import lax
from jax.experimental import pallas as pl
from jax.experimental.pallas import tpu as pltpu
from jax.sharding import PartitionSpec as P

MESH = pl.DeviceIdType.MESH
F32, BF16 = jnp.float32, jnp.bfloat16
GROUPS = ((0, 512), (512, 512), (1024, 640))
NG = len(GROUPS)
SLICE = 104


def flip(v, b):
    return v + b - 2 * b * lax.rem(lax.div(v, b), 2)


def dot_nt(a, b):
    return lax.dot_general(a, b, (((1,), (1,)), ((), ())), preferred_element_type=F32)


def kernel(
    grad, codes, scale, down, up, act, out, comp,
    gbuf, codes_v, scale_v, down_v, up_v, act_v, lhs, acc, psend, precv, xsend, xrecv, zsend, zrecv,
    low, lprecv, lxrecv, lzrecv, cblk, cprecv, cxrecv, czrecv,
    lsem, gzs, gzr, gys, gyr, pss, psr, xss, xsr, zss, zsr,
    lps, lpr, lxs, lxr, lzs, lzr, cps, cpr, cxs, cxr, czs, czr,
):
    row, col = lax.axis_index("row"), lax.axis_index("col")
    core, zh, x = lax.rem(row, 2), lax.rem(lax.div(row, 2), 2), lax.div(row, 4)
    y, zl = lax.rem(col, 4), lax.div(col, 4)

    def at_row(x_, zh_, core_):
        return {"row": x_ * 4 + zh_ * 2 + core_, "col": col}

    def at_col(zl_, y_):
        return {"row": row, "col": zl_ * 4 + y_}

    mate = at_row(x, zh, 1 - core)
    far = at_row(x, 1 - zh, core)
    xs = [lax.rem(x + j, 4) for j in (1, 2, 3)]
    x_peer = [at_row(v, zh, core) for v in xs]
    y_peer = [at_col(zl, lax.rem(y + j, 4)) for j in (1, 2, 3)]
    z_peer = {b: at_col(flip(zl, b), y) for b in (1, 2, 4)}

    def rc(src, dst, ss, rs, dev):
        return pltpu.make_async_remote_copy(
            src_ref=src, dst_ref=dst, send_sem=ss, recv_sem=rs, device_id=dev, device_id_type=MESH
        )

    local = [
        pltpu.make_async_copy(s, d, lsem.at[i])
        for i, (s, d) in enumerate(
            ((grad, gbuf.at[col]), (scale, scale_v), (up, up_v), (codes, codes_v), (down, down_v), (act, act_v))
        )
    ]
    for c in local:
        c.start()

    barrier = pltpu.get_barrier_semaphore()
    peers = [mate, far, *x_peer, *y_peer, *z_peer.values()]
    for p in peers:
        pl.semaphore_signal(barrier, inc=1, device_id=p, device_id_type=MESH)
    pl.semaphore_wait(barrier, len(peers))
    local[0].wait()

    sends = []

    def zmap(m):
        v = zl
        for b in (1, 2, 4):
            if m & b:
                v = flip(v, b)
        return v

    def pass_on(m, bits):
        k = zmap(m)
        c = k * 4 + y
        for b in bits:
            d = rc(gbuf.at[c], gbuf.at[c], gzs.at[m ^ b], gzr.at[m ^ b], z_peer[b])
            d.start()
            sends.append(d)
        for j in range(3):
            d = rc(gbuf.at[c], gbuf.at[c], gys.at[k, j], gyr.at[k, j], y_peer[j])
            d.start()
            sends.append(d)

    def z_wait(m):
        c = zmap(m) * 4 + y
        rc(gbuf.at[c], gbuf.at[c], gzs.at[m], gzr.at[m], z_peer[1]).wait_recv()

    pass_on(0, (4, 2, 1))
    for m, bits in ((4, (2, 1)), (2, (1,)), (1, ()), (6, (1,)), (5, ()), (3, ()), (7, ())):
        z_wait(m)
        pass_on(m, bits)

    for c in local[1:3]:
        c.wait()

    def y_wait(par):
        for v in range(4):
            k = 2 * v + par
            for j in range(3):
                c = k * 4 + lax.rem(y + 3 - j, 4)
                rc(gbuf.at[c], gbuf.at[c], gys.at[k, j], gyr.at[k, j], y_peer[j]).wait_recv()

    def prepare(q, par):
        for i, c_ in enumerate((1 - core, core)):
            for v in range(4):
                g = gbuf[pl.ds((2 * v + par) * 4 + 2 * c_, 2)].reshape(32, 1024)
                low[q, i, v, :, 0:32] = dot_nt(up_v[...], g)
                lhs[i, v * 32 : v * 32 + 32, :] = (g.astype(F32) * scale_v[...]).astype(BF16)

    def pair_copies(q):
        return [
            rc(psend.at[q, :, :, pl.ds(n, w)], precv.at[q, :, :, pl.ds(n, w)], pss.at[q, s], psr.at[q, s], mate)
            for s, (n, w) in enumerate(GROUPS)
        ]

    def low_pair(q):
        return rc(low.at[q, 0], lprecv.at[q], lps.at[q], lpr.at[q], mate)

    def x_copies(q, s):
        n, w = GROUPS[s]
        return [
            rc(
                xsend.at[q, xs[j], :, pl.ds(n, w)], xrecv.at[q, j, :, pl.ds(n, w)],
                xss.at[q, s, j], xsr.at[q, s, j], x_peer[j],
            )
            for j in range(3)
        ]

    def low_x(q):
        return [
            rc(low.at[q, 1, xs[j]], lxrecv.at[q, j], lxs.at[q, j], lxr.at[q, j], x_peer[j]) for j in range(3)
        ]

    def multiply(q):
        low_pair(q).start()
        copies = pair_copies(q)
        for s, (n, w) in enumerate(GROUPS):
            r = dot_nt(lhs[0], codes_v[n : n + w, :])
            psend[q, :, :, n : n + w] = r.astype(BF16).reshape(4, 32, w)
            copies[s].start()
        for s, (n, w) in enumerate(GROUPS):
            acc[q, :, :, n : n + w] = dot_nt(lhs[1], codes_v[n : n + w, :]).reshape(4, 32, w)

    def to_x(q):
        low_pair(q).wait_recv()
        low[q, 1] = low[q, 1] + lprecv[q]
        for d in low_x(q):
            d.start()
        copies = pair_copies(q)
        for s, (n, w) in enumerate(GROUPS):
            copies[s].wait_recv()
            v = acc[q, :, :, n : n + w] + precv[q, :, :, n : n + w].astype(F32)
            acc[q, :, :, n : n + w] = v
            xsend[q, :, :, n : n + w] = v.astype(BF16)
            for d in x_copies(q, s):
                d.start()

    def x_sum(q, s):
        n, w = GROUPS[s]
        for d in x_copies(q, s):
            d.wait_recv()
        v = acc[q, pl.ds(x, 1), :, n : n + w].reshape(32, w)
        for j in range(3):
            v = v + xrecv[q, j, :, n : n + w].astype(F32)
        return v

    def low_sum(q):
        for d in low_x(q):
            d.wait_recv()
        v = low[q, 1, pl.ds(x, 1)].reshape(16, 128)
        for j in range(3):
            v = v + lxrecv[q, j]
        return v

    low_far = rc(low.at[0, 0, 0], lzrecv, lzs, lzr, far)
    z_copies = [
        rc(zsend.at[:, pl.ds(n, w)], zrecv.at[:, pl.ds(n, w)], zss.at[s], zsr.at[s], far)
        for s, (n, w) in enumerate(GROUPS)
    ]

    low[...] = jnp.zeros_like(low)
    y_wait(1 - zh)
    prepare(0, 1 - zh)
    local[3].wait()
    multiply(0)
    to_x(0)
    y_wait(zh)
    prepare(1, zh)
    multiply(1)
    low_pair(0).wait_send()
    low[0, 0, 0] = low_sum(0)
    low_far.start()
    for s, (n, w) in enumerate(GROUPS):
        zsend[:, n : n + w] = x_sum(0, s).astype(BF16)
        z_copies[s].start()
    to_x(1)

    v = low_sum(1)
    low_far.wait_recv()
    rounded = (v + lzrecv[...]).astype(BF16)[:, 0:32]
    for c in local[4:]:
        c.wait()
    part = 0.5 * jnp.dot(rounded, act_v[...], preferred_element_type=F32)
    for r in range(16):
        start = r * SLICE
        base, off = start // 128 * 128, start % 128
        if off + SLICE <= 128:
            b = part[:, base : base + 128]
            b = pltpu.roll(b, (128 - off) % 128, 1) if off else b
        else:
            b = pltpu.roll(part[:, base : base + 256], 256 - off, 1)[:, 0:128]
        cblk[r % 2, r // 4, (r // 2) % 2] = b
    c_pair = rc(cblk.at[1 - core], cprecv, cps, cpr, mate)
    c_pair.start()

    for s, (n, w) in enumerate(GROUPS):
        term = lax.dot_general(
            rounded, down_v[:, n : n + w], (((0,), (0,)), ((), ())), preferred_element_type=F32
        )
        acc[0, 0, :, n : n + w] = x_sum(1, s) + 0.5 * term
        if s == 0:
            c_pair.wait_recv()
            cblk[pl.ds(core, 1)] = cblk[pl.ds(core, 1)] + cprecv[...][None]
            c_x = [rc(cblk.at[core, xs[j]], cxrecv.at[j], cxs.at[j], cxr.at[j], x_peer[j]) for j in range(3)]
            for d in c_x:
                d.start()

    for d in c_x:
        d.wait_recv()
    v = cblk[pl.ds(core, 1), pl.ds(x, 1)].reshape(2, 16, 128)
    for j in range(3):
        v = v + cxrecv[j]
    c_pair.wait_send()
    cblk[pl.ds(1 - core, 1), 0] = v[None]
    c_far = rc(cblk.at[1 - core, 0, 1 - zh], czrecv, czs, czr, far)
    c_far.start()

    for s, (n, w) in enumerate(GROUPS):
        z_copies[s].wait_recv()
        out[:, n : n + w] = (acc[0, 0, :, n : n + w] + zrecv[:, n : n + w].astype(F32)).astype(BF16)
    c_far.wait_recv()
    keep = cblk[pl.ds(1 - core, 1), 0, pl.ds(zh, 1)].reshape(16, 128)
    comp[...] = (keep + czrecv[...])[:, 0:SLICE]

    for d in sends:
        d.wait_send()
    low_pair(1).wait_send()
    for q in range(2):
        for d in pair_copies(q) + low_x(q):
            d.wait_send()
        for s in range(NG):
            for d in x_copies(q, s):
                d.wait_send()
    for d in [low_far, c_far, *c_x, *z_copies]:
        d.wait_send()


def on_device(grad, codes, scale, down, up, act):
    hidden, width = codes.shape
    any_ = pl.BlockSpec(memory_space=pl.ANY)
    vmem = pl.BlockSpec(memory_space=pltpu.VMEM)
    dma = pltpu.SemaphoreType.DMA
    out, comp = pl.pallas_call(
        kernel,
        out_shape=(
            jax.ShapeDtypeStruct((32, hidden), BF16),
            jax.ShapeDtypeStruct((16, SLICE), F32),
        ),
        in_specs=[any_] * 6,
        out_specs=(vmem, vmem),
        scratch_shapes=[
            pltpu.VMEM((32, 16, width), BF16),
            pltpu.VMEM((hidden, width), BF16),
            pltpu.VMEM((1, width), F32),
            pltpu.VMEM((16, hidden), BF16),
            pltpu.VMEM((16, width), BF16),
            pltpu.VMEM((32, hidden), BF16),
            pltpu.VMEM((2, 128, width), BF16),
            pltpu.VMEM((2, 4, 32, hidden), F32),
            pltpu.VMEM((2, 4, 32, hidden), BF16),
            pltpu.VMEM((2, 4, 32, hidden), BF16),
            pltpu.VMEM((2, 4, 32, hidden), BF16),
            pltpu.VMEM((2, 3, 32, hidden), BF16),
            pltpu.VMEM((32, hidden), BF16),
            pltpu.VMEM((32, hidden), BF16),
            pltpu.VMEM((2, 2, 4, 16, 128), F32),
            pltpu.VMEM((2, 4, 16, 128), F32),
            pltpu.VMEM((2, 3, 16, 128), F32),
            pltpu.VMEM((16, 128), F32),
            pltpu.VMEM((2, 4, 2, 16, 128), F32),
            pltpu.VMEM((4, 2, 16, 128), F32),
            pltpu.VMEM((3, 2, 16, 128), F32),
            pltpu.VMEM((16, 128), F32),
            dma((6,)),
            dma((8,)), dma((8,)), dma((8, 3)), dma((8, 3)),
            dma((2, NG)), dma((2, NG)), dma((2, NG, 3)), dma((2, NG, 3)), dma((NG,)), dma((NG,)),
            dma((2,)), dma((2,)), dma((2, 3)), dma((2, 3)), dma, dma,
            dma, dma, dma((3,)), dma((3,)), dma, dma,
        ],
        compiler_params=pltpu.CompilerParams(
            collective_id=0, has_side_effects=True, vmem_limit_bytes=60 * 2**20
        ),
        cost_estimate=pl.CostEstimate(flops=2 * 512 * hidden * width, bytes_accessed=4 * 2**20, transcendentals=0),
    )(grad, codes, scale.reshape(1, width), down, up, act)
    return out, comp


def solution(mesh):
    return jax.shard_map(
        on_device,
        mesh=mesh,
        in_specs=(
            P("col", "row"),
            P("col", "row"),
            P("row"),
            P(None, "col"),
            P(None, "row"),
            P("row", "col"),
        ),
        out_specs=(P("row", "col"), P(None, ("col", "row"))),
        check_vma=False,
    )
```

```python
import jax
import jax.numpy as jnp
from jax import lax
from jax.experimental import pallas as pl
from jax.experimental.pallas import tpu as pltpu
from jax.sharding import PartitionSpec as P

MESH = pl.DeviceIdType.MESH
F32, BF16 = jnp.float32, jnp.bfloat16
GROUPS = ((0, 768), (768, 896))
NG = len(GROUPS)
SLICE = 104
RANK = 16


def flip(v, b):
    return v + b - 2 * b * lax.rem(lax.div(v, b), 2)


def dot_nt(a, b):
    return lax.dot_general(a, b, (((1,), (1,)), ((), ())), preferred_element_type=F32)


def dot_tn(a, b):
    return lax.dot_general(a, b, (((0,), (0,)), ((), ())), preferred_element_type=F32)


def kernel(
    grad, codes, scale, down, up, act, out, comp,
    gbuf, codes_v, codes_t, scale_v, down_v, up_v, act_v, lhs, acc, psend, precv, xsend, xrecv, zsend, zrecv, total,
    lsum, lmate, lx, lfar, low, cblk, cprecv, cxrecv, czsend, czrecv,
    far_in, lsem, gzs, gzr, gys, gyr, pss, psr, xss, xsr, zss, zsr,
    lps, lpr, lxs, lxr, lfs, lfr, lys, lyr, lzs, lzr, cps, cpr, cxs, cxr, czs, czr,
):
    row, col = lax.axis_index("row"), lax.axis_index("col")
    core, zh, x = lax.rem(row, 2), lax.rem(lax.div(row, 2), 2), lax.div(row, 4)
    y, zl = lax.rem(col, 4), lax.div(col, 4)

    def at_row(x_, zh_, core_):
        return {"row": x_ * 4 + zh_ * 2 + core_, "col": col}

    def at_col(zl_, y_):
        return {"row": row, "col": zl_ * 4 + y_}

    def zmap(m):
        v = zl
        for b in (1, 2, 4):
            if m & b:
                v = flip(v, b)
        return v

    mate = at_row(x, zh, 1 - core)
    far = at_row(x, 1 - zh, core)
    cross = {"row": x * 4 + (1 - zh) * 2 + core, "col": zmap(4) * 4 + y}
    xs = [lax.rem(x + j, 4) for j in (1, 2, 3)]
    x_peer = [at_row(v, zh, core) for v in xs]
    y_peer = [at_col(zl, lax.rem(y + j, 4)) for j in (1, 2, 3)]
    z_peer = {m: at_col(zmap(m), y) for m in (1, 2, 3, 4)}

    def rc(src, dst, ss, rs, dev):
        return pltpu.make_async_remote_copy(
            src_ref=src, dst_ref=dst, send_sem=ss, recv_sem=rs, device_id=dev, device_id_type=MESH
        )

    local = [
        pltpu.make_async_copy(s, d, lsem.at[i])
        for i, (s, d) in enumerate(
            ((grad, gbuf.at[col]), (scale, scale_v), (up, up_v), (codes, codes_v), (down, down_v), (act, act_v))
        )
    ]
    for c in local:
        c.start()

    barrier = pltpu.get_barrier_semaphore()
    peers = [z_peer[4], cross, z_peer[3], z_peer[2], z_peer[1], *x_peer, *y_peer, mate]
    for p in peers:
        pl.semaphore_signal(barrier, inc=1, device_id=p, device_id_type=MESH)
    local[0].wait()
    local[2].wait()
    lsum[...] = jnp.zeros_like(lsum)
    lsum[0, :, 0:RANK] = dot_nt(gbuf[pl.ds(col, 1)].reshape(16, -1), up_v[...])
    low_mate = rc(lsum.at[0], lmate, lps, lpr, mate)
    low_x = [rc(lsum.at[1], lx.at[j], lxs.at[j], lxr.at[j], x_peer[j]) for j in range(3)]
    low_far = rc(lsum.at[2], lfar, lfs, lfr, far)
    pl.semaphore_wait(barrier, len(peers))
    pl.semaphore_signal(far_in, inc=1, device_id=z_peer[4], device_id_type=MESH)

    sends = []

    def pass_on(m, bits):
        k = zmap(m)
        c = k * 4 + y
        for b in bits:
            d = rc(gbuf.at[c], gbuf.at[c], gzs.at[m ^ b], gzr.at[m ^ b], z_peer[b])
            d.start()
            sends.append(d)
        for j in range(3):
            d = rc(gbuf.at[c], gbuf.at[c], gys.at[k, j], gyr.at[k, j], y_peer[j])
            d.start()
            sends.append(d)

    def z_wait(m):
        c = zmap(m) * 4 + y
        rc(gbuf.at[c], gbuf.at[c], gzs.at[m], gzr.at[m], z_peer[1]).wait_recv()

    pass_on(0, (4, 3, 2, 1))
    low_mate.start()
    local[3].wait()
    for n in range(0, codes_v.shape[0], 128):
        codes_t[:, n : n + 128] = codes_v[n : n + 128, :].T
    z_wait(1)
    pass_on(1, ())
    low_mate.wait_recv()
    lsum[1] = lsum[0] + lmate[...]
    for d in low_x:
        d.start()
    for m in (2, 3):
        z_wait(m)
        pass_on(m, ())
    lsum[2] = lsum[1]
    for j in range(3):
        low_x[j].wait_recv()
        lsum[2] += lx[j]
    pl.semaphore_wait(far_in, 1)
    low_far.start()
    z_wait(4)
    pass_on(4, (3, 2, 1))
    for m in (5, 6, 7):
        z_wait(m)
        pass_on(m, ())

    at_source = zl == 2 * x + zh
    is_source = [at_source & (lax.div(y, 2) == core) & (lax.rem(y, 2) == b) for b in (0, 1)]
    low_y = [[rc(low.at[b], low.at[b], lys.at[b, j], lyr.at[b], y_peer[j]) for j in range(3)] for b in (0, 1)]
    low_z = [rc(low, low, lzs.at[m], lzr, at_col(zmap(m), y)) for m in range(1, 8)]

    def low_to_y():
        low_far.wait_recv()
        whole = (lsum[2] + lfar[...]).astype(BF16)
        for b in (0, 1):

            def give(b=b):
                low[b] = whole
                for d in low_y[b]:
                    d.start()

            pl.when(is_source[b])(give)

    def low_to_z():
        for b in (0, 1):
            pl.when(at_source & jnp.logical_not(is_source[b]))(lambda b=b: low_y[b][0].wait_recv())

        def give():
            for d in low_z:
                d.start()

        pl.when(at_source)(give)

    local[1].wait()

    half = lax.div(zl, 4)
    half_of = [half, 1 - half, half, 1 - half]
    parity_of = [1 - zh, 1 - zh, zh, zh]
    inside = [lax.div(x, 2) == h for h in half_of]

    def pair_copies(t):
        return [
            rc(psend.at[t, :, :, pl.ds(n, w)], precv.at[t, :, :, pl.ds(n, w)], pss.at[t, s], psr.at[t, s], mate)
            for s, (n, w) in enumerate(GROUPS)
        ]

    def x_copy(t, s, i):
        n, w = GROUPS[s]
        d = 2 * half_of[t] + i
        j = lax.rem(d - x + 3, 4)
        return rc(
            xsend.at[t, i, :, pl.ds(n, w)], xrecv.at[t // 2, j, :, pl.ds(n, w)],
            xss.at[t, s, i], xsr.at[t // 2, s, j], at_row(d, zh, core),
        )

    def leaves(t, i):
        return x != 2 * half_of[t] + i

    def multiply(t):
        for v in range(2):
            k = 4 * half_of[t] + 2 * v + parity_of[t]
            for j in range(3):
                c = k * 4 + lax.rem(y + 3 - j, 4)
                rc(gbuf.at[c], gbuf.at[c], gys.at[k, j], gyr.at[k, j], y_peer[j]).wait_recv()
        for i, c_ in enumerate((1 - core, core)):
            for v in range(2):
                k = 4 * half_of[t] + 2 * v + parity_of[t]
                g = gbuf[pl.ds(k * 4 + 2 * c_, 2)].reshape(32, 1024)
                n = i * 64 + v * 32
                lhs[t, n : n + 32, :] = (g.astype(F32) * scale_v[...]).astype(BF16)
        copies = pair_copies(t)
        for s, (n, w) in enumerate(GROUPS):
            r = jnp.dot(lhs[t], codes_t[:, n : n + w], preferred_element_type=F32)
            psend[t, :, :, n : n + w] = r[0:64].astype(BF16).reshape(2, 32, w)
            copies[s].start()
            acc[t, :, :, n : n + w] = r[64:128].reshape(2, 32, w)

    def to_x(t):
        copies = pair_copies(t)
        for s, (n, w) in enumerate(GROUPS):
            copies[s].wait_recv()
            v = acc[t, :, :, n : n + w] + precv[t, :, :, n : n + w].astype(F32)
            acc[t, :, :, n : n + w] = v
            xsend[t, :, :, n : n + w] = v.astype(BF16)
            for i in range(2):
                pl.when(leaves(t, i))(lambda s=s, i=i: x_copy(t, s, i).start())

    mine = lax.rem(x, 2)

    def x_sum(t, s):
        q = t // 2
        n, w = GROUPS[s]
        for j in range(3):
            rc(
                xrecv.at[q, j, :, pl.ds(n, w)], xrecv.at[q, j, :, pl.ds(n, w)],
                xss.at[t, s, 0], xsr.at[q, s, j], x_peer[j],
            ).wait_recv()
        v = acc[t, pl.ds(mine, 1), :, n : n + w].reshape(32, w)
        for j in range(3):
            v = v + xrecv[q, j, :, n : n + w].astype(F32)
        return v

    z_copies = [
        rc(zsend.at[:, pl.ds(n, w)], zrecv.at[:, pl.ds(n, w)], zss.at[s], zsr.at[s], far)
        for s, (n, w) in enumerate(GROUPS)
    ]

    def to_far(t):
        for s, (n, w) in enumerate(GROUPS):
            zsend[:, n : n + w] = x_sum(t, s).astype(BF16)
            z_copies[s].start()

    def keep(t, s):
        n, w = GROUPS[s]
        total[:, n : n + w] = x_sum(t, s)

    low_to_y()
    multiply(0)
    to_x(0)
    low_to_z()
    multiply(2)
    multiply(1)
    to_x(1)
    multiply(3)
    pl.when(inside[0])(lambda: to_far(0))
    to_x(2)
    to_x(3)

    pl.when(jnp.logical_not(at_source))(lambda: low_z[0].wait_recv())
    rounded = low[...].reshape(32, 128)[:, 0:RANK]
    for c in local[4:]:
        c.wait()
    part = 0.5 * dot_tn(rounded, act_v[...])
    for r in range(16):
        start = r * SLICE
        base, off = start // 128 * 128, start % 128
        if off + SLICE <= 128:
            b = part[:, base : base + 128]
            b = pltpu.roll(b, (128 - off) % 128, 1) if off else b
        else:
            b = pltpu.roll(part[:, base : base + 256], 256 - off, 1)[:, 0:128]
        cblk[r % 2, r // 4, (r // 2) % 2] = b
    c_pair = rc(cblk.at[1 - core], cprecv, cps, cpr, mate)
    c_pair.start()
    pl.when(inside[1])(lambda: to_far(1))
    c_pair.wait_recv()
    cblk[pl.ds(core, 1)] = cblk[pl.ds(core, 1)] + cprecv[...][None]
    c_x = [rc(cblk.at[core, xs[j]], cxrecv.at[j], cxs.at[j], cxr.at[j], x_peer[j]) for j in range(3)]
    for d in c_x:
        d.start()

    def comp_far():
        for d in c_x:
            d.wait_recv()
        v = cblk[pl.ds(core, 1), pl.ds(x, 1)].reshape(2, 16, 128)
        for j in range(3):
            v = v + cxrecv[j]
        czsend[...] = v
        c_far.start()

    c_far = rc(czsend.at[1 - zh], czrecv, czs, czr, far)
    for s, (n, w) in enumerate(GROUPS):
        term = jnp.dot(rounded, down_v[:, n : n + w], preferred_element_type=F32)
        for t in (2, 3):
            pl.when(inside[t])(lambda t=t, s=s: keep(t, s))
        total[:, n : n + w] += 0.5 * term
        if s == 0:
            comp_far()

    for s, (n, w) in enumerate(GROUPS):
        z_copies[s].wait_recv()
        out[:, n : n + w] = (total[:, n : n + w] + zrecv[:, n : n + w].astype(F32)).astype(BF16)
    c_far.wait_recv()
    comp[...] = (czsend[pl.ds(zh, 1)].reshape(16, 128) + czrecv[...])[:, 0:SLICE]

    for d in sends:
        d.wait_send()
    for t in range(4):
        for d in pair_copies(t):
            d.wait_send()
        for i in range(2):

            def sent(t=t, i=i):
                for s in range(NG):
                    x_copy(t, s, i).wait_send()

            pl.when(leaves(t, i))(sent)
    for d in [low_mate, *low_x, low_far, c_pair, c_far, *c_x, *z_copies]:
        d.wait_send()
    for b in (0, 1):
        pl.when(is_source[b])(lambda b=b: [d.wait_send() for d in low_y[b]] and None)
    pl.when(at_source)(lambda: [d.wait_send() for d in low_z] and None)


def write_out(a, b, c, d, sems):
    copies = [pltpu.make_async_copy(a, c, sems.at[0]), pltpu.make_async_copy(b, d, sems.at[1])]
    for v in copies:
        v.start()
    for v in copies:
        v.wait()


def on_device(grad, codes, scale, down, up, act):
    hidden, width = codes.shape
    any_ = pl.BlockSpec(memory_space=pl.ANY)
    vmem = pl.BlockSpec(memory_space=pltpu.VMEM)
    dma = pltpu.SemaphoreType.DMA
    out, comp = pl.pallas_call(
        kernel,
        out_shape=(
            jax.ShapeDtypeStruct((32, hidden), BF16),
            jax.ShapeDtypeStruct((16, SLICE), F32),
        ),
        in_specs=[any_] * 6,
        out_specs=(vmem, vmem),
        scratch_shapes=[
            pltpu.VMEM((32, 16, width), BF16),
            pltpu.VMEM((hidden, width), BF16),
            pltpu.VMEM((width, hidden), BF16),
            pltpu.VMEM((1, width), F32),
            pltpu.VMEM((16, hidden), BF16),
            pltpu.VMEM((16, width), BF16),
            pltpu.VMEM((32, hidden), BF16),
            pltpu.VMEM((4, 128, width), BF16),
            pltpu.VMEM((4, 2, 32, hidden), F32),
            pltpu.VMEM((4, 2, 32, hidden), BF16),
            pltpu.VMEM((4, 2, 32, hidden), BF16),
            pltpu.VMEM((4, 2, 32, hidden), BF16),
            pltpu.VMEM((2, 3, 32, hidden), BF16),
            pltpu.VMEM((32, hidden), BF16),
            pltpu.VMEM((32, hidden), BF16),
            pltpu.VMEM((32, hidden), F32),
            pltpu.VMEM((3, 16, 128), F32),
            pltpu.VMEM((16, 128), F32),
            pltpu.VMEM((3, 16, 128), F32),
            pltpu.VMEM((16, 128), F32),
            pltpu.VMEM((2, 16, 128), BF16),
            pltpu.VMEM((2, 4, 2, 16, 128), F32),
            pltpu.VMEM((4, 2, 16, 128), F32),
            pltpu.VMEM((3, 2, 16, 128), F32),
            pltpu.VMEM((2, 16, 128), F32),
            pltpu.VMEM((16, 128), F32),
            pltpu.SemaphoreType.REGULAR,
            dma((6,)),
            dma((8,)), dma((8,)), dma((8, 3)), dma((8, 3)),
            dma((4, NG)), dma((4, NG)), dma((4, NG, 2)), dma((2, NG, 3)), dma((NG,)), dma((NG,)),
            dma, dma, dma((3,)), dma((3,)), dma, dma, dma((2, 3)), dma((2,)), dma((8,)), dma,
            dma, dma, dma((3,)), dma((3,)), dma, dma,
        ],
        compiler_params=pltpu.CompilerParams(
            collective_id=0, has_side_effects=True, vmem_limit_bytes=60 * 2**20
        ),
        cost_estimate=pl.CostEstimate(flops=2 * 512 * hidden * width, bytes_accessed=4 * 2**20, transcendentals=0),
    )(grad, codes, scale.reshape(1, width), down, up, act)
    return tuple(
        pl.pallas_call(
            write_out,
            out_shape=(
                jax.ShapeDtypeStruct((32, hidden), BF16),
                jax.ShapeDtypeStruct((16, SLICE), F32),
            ),
            in_specs=[vmem, vmem],
            out_specs=(any_, any_),
            scratch_shapes=[dma((2,))],
            compiler_params=pltpu.CompilerParams(has_side_effects=True),
        )(out, comp)
    )


def solution(mesh):
    return jax.shard_map(
        on_device,
        mesh=mesh,
        in_specs=(
            P("col", "row"),
            P("col", "row"),
            P("row"),
            P(None, "col"),
            P(None, "row"),
            P("row", "col"),
        ),
        out_specs=(P("row", "col"), P(None, ("col", "row"))),
        check_vma=False,
    )
```

```python
import jax
import jax.numpy as jnp
from jax import lax
from jax.experimental import pallas as pl
from jax.experimental.pallas import tpu as pltpu
from jax.sharding import PartitionSpec as P

MESH = pl.DeviceIdType.MESH
F32, BF16 = jnp.float32, jnp.bfloat16
GROUPS = ((0, 768), (768, 896))
NG = len(GROUPS)
SLICE = 104
RANK = 16


def flip(v, b):
    return v + b - 2 * b * lax.rem(lax.div(v, b), 2)


def dot_nt(a, b):
    return lax.dot_general(a, b, (((1,), (1,)), ((), ())), preferred_element_type=F32)


def dot_tn(a, b):
    return lax.dot_general(a, b, (((0,), (0,)), ((), ())), preferred_element_type=F32)


def kernel(
    grad, codes, scale, down, up, act, out, comp,
    gbuf, codes_v, codes_t, scale_v, down_v, up_v, act_v, lhs, acc, psend, precv, xsend, xrecv, zsend, zrecv, total,
    lsum, lmate, lx, lfar, low, cblk, cprecv, cxrecv, czsend, czrecv,
    far_in, lsem, gzs, gzr, gys, gyr, pss, psr, xss, xsr, zss, zsr,
    lps, lpr, lxs, lxr, lfs, lfr, lys, lyr, lzs, lzr, cps, cpr, cxs, cxr, czs, czr,
):
    row, col = lax.axis_index("row"), lax.axis_index("col")
    core, zh, x = lax.rem(row, 2), lax.rem(lax.div(row, 2), 2), lax.div(row, 4)
    y, zl = lax.rem(col, 4), lax.div(col, 4)

    def at_row(x_, zh_, core_):
        return {"row": x_ * 4 + zh_ * 2 + core_, "col": col}

    def at_col(zl_, y_):
        return {"row": row, "col": zl_ * 4 + y_}

    def zmap(m):
        v = zl
        for b in (1, 2, 4):
            if m & b:
                v = flip(v, b)
        return v

    mate = at_row(x, zh, 1 - core)
    far = at_row(x, 1 - zh, core)
    cross = {"row": x * 4 + (1 - zh) * 2 + core, "col": zmap(4) * 4 + y}
    xs = [lax.rem(x + j, 4) for j in (1, 2, 3)]
    x_peer = [at_row(v, zh, core) for v in xs]
    y_peer = [at_col(zl, lax.rem(y + j, 4)) for j in (1, 2, 3)]
    z_peer = {m: at_col(zmap(m), y) for m in (1, 2, 3, 4)}

    def rc(src, dst, ss, rs, dev):
        return pltpu.make_async_remote_copy(
            src_ref=src, dst_ref=dst, send_sem=ss, recv_sem=rs, device_id=dev, device_id_type=MESH
        )

    local = [
        pltpu.make_async_copy(s, d, lsem.at[i])
        for i, (s, d) in enumerate(
            ((grad, gbuf.at[col]), (scale, scale_v), (up, up_v), (codes, codes_v), (down, down_v), (act, act_v))
        )
    ]
    for c in local:
        c.start()

    barrier = pltpu.get_barrier_semaphore()
    peers = [z_peer[4], cross, z_peer[3], z_peer[2], z_peer[1], *x_peer, *y_peer, mate]
    for p in peers:
        pl.semaphore_signal(barrier, inc=1, device_id=p, device_id_type=MESH)
    local[0].wait()
    local[2].wait()
    lsum[...] = jnp.zeros_like(lsum)
    lsum[0, :, 0:RANK] = dot_nt(gbuf[pl.ds(col, 1)].reshape(16, -1), up_v[...])
    low_mate = rc(lsum.at[0], lmate, lps, lpr, mate)
    low_x = [rc(lsum.at[1], lx.at[j], lxs.at[j], lxr.at[j], x_peer[j]) for j in range(3)]
    low_far = rc(lsum.at[2], lfar, lfs, lfr, far)
    pl.semaphore_wait(barrier, len(peers))
    pl.semaphore_signal(far_in, inc=1, device_id=z_peer[4], device_id_type=MESH)

    sends = []

    def pass_on(m, bits):
        k = zmap(m)
        c = k * 4 + y
        for b in bits:
            d = rc(gbuf.at[c], gbuf.at[c], gzs.at[m ^ b], gzr.at[m ^ b], z_peer[b])
            d.start()
            sends.append(d)
        for j in range(3):
            d = rc(gbuf.at[c], gbuf.at[c], gys.at[k, j], gyr.at[k, j], y_peer[j])
            d.start()
            sends.append(d)

    def z_wait(m):
        c = zmap(m) * 4 + y
        rc(gbuf.at[c], gbuf.at[c], gzs.at[m], gzr.at[m], z_peer[1]).wait_recv()

    odd = 1 - lax.rem(zl + zh, 2)

    def pass_three(base):
        even_k, odd_k = [zmap(base + 2)], [zmap(base + 1), zmap(base + 3)]
        for m, k in (
            (base + 2 - odd, odd * odd_k[0] + (1 - odd) * even_k[0]),
            (base + 1 + 2 * odd, odd * odd_k[1] + (1 - odd) * odd_k[0]),
            (base + 3 - odd, odd * even_k[0] + (1 - odd) * odd_k[1]),
        ):
            c = k * 4 + y
            rc(gbuf.at[c], gbuf.at[c], gzs.at[m], gzr.at[m], z_peer[1]).wait_recv()
            for j in range(3):
                d = rc(gbuf.at[c], gbuf.at[c], gys.at[k, j], gyr.at[k, j], y_peer[j])
                d.start()
                sends.append(d)

    pass_on(0, (4, 3, 2, 1))
    low_mate.start()
    local[1].wait()
    local[3].wait()
    for n in range(0, codes_v.shape[0], 128):
        codes_t[:, n : n + 128] = codes_v[n : n + 128, :].T
    low_mate.wait_recv()
    lsum[1] = lsum[0] + lmate[...]
    for d in low_x:
        d.start()
    pass_three(0)
    lsum[2] = lsum[1]
    for j in range(3):
        low_x[j].wait_recv()
        lsum[2] += lx[j]
    pl.semaphore_wait(far_in, 1)
    low_far.start()
    z_wait(4)
    pass_on(4, (3, 2, 1))

    at_source = zl == 2 * x + zh
    is_source = [at_source & (lax.div(y, 2) == core) & (lax.rem(y, 2) == b) for b in (0, 1)]
    low_y = [[rc(low.at[b], low.at[b], lys.at[b, j], lyr.at[b], y_peer[j]) for j in range(3)] for b in (0, 1)]
    low_z = [rc(low, low, lzs.at[m], lzr, at_col(zmap(m), y)) for m in range(1, 8)]

    def low_to_y():
        low_far.wait_recv()
        whole = (lsum[2] + lfar[...]).astype(BF16)
        for b in (0, 1):

            def give(b=b):
                low[b] = whole
                for d in low_y[b]:
                    d.start()

            pl.when(is_source[b])(give)

    def low_to_z():
        for b in (0, 1):
            pl.when(at_source & jnp.logical_not(is_source[b]))(lambda b=b: low_y[b][0].wait_recv())

        def give():
            for d in low_z:
                d.start()

        pl.when(at_source)(give)

    half = lax.div(zl, 4)
    half_of = [half, 1 - half, half, 1 - half]
    parity_of = [1 - zh, 1 - zh, zh, zh]
    inside = [lax.div(x, 2) == h for h in half_of]

    def pair_copies(t):
        return [
            rc(psend.at[t, :, :, pl.ds(n, w)], precv.at[t, :, :, pl.ds(n, w)], pss.at[t, s], psr.at[t, s], mate)
            for s, (n, w) in enumerate(GROUPS)
        ]

    def x_copy(t, s, i):
        n, w = GROUPS[s]
        d = 2 * half_of[t] + i
        j = lax.rem(d - x + 3, 4)
        return rc(
            xsend.at[t, i, :, pl.ds(n, w)], xrecv.at[t // 2, j, :, pl.ds(n, w)],
            xss.at[t, s, i], xsr.at[t // 2, s, j], at_row(d, zh, core),
        )

    def leaves(t, i):
        return x != 2 * half_of[t] + i

    def multiply(t):
        for v in range(2):
            k = 4 * half_of[t] + 2 * v + parity_of[t]
            for j in range(3):
                c = k * 4 + lax.rem(y + 3 - j, 4)
                rc(gbuf.at[c], gbuf.at[c], gys.at[k, j], gyr.at[k, j], y_peer[j]).wait_recv()
        for i, c_ in enumerate((1 - core, core)):
            for v in range(2):
                k = 4 * half_of[t] + 2 * v + parity_of[t]
                g = gbuf[pl.ds(k * 4 + 2 * c_, 2)].reshape(32, 1024)
                n = i * 64 + v * 32
                lhs[t, n : n + 32, :] = (g.astype(F32) * scale_v[...]).astype(BF16)
        copies = pair_copies(t)
        for s, (n, w) in enumerate(GROUPS):
            r = jnp.dot(lhs[t], codes_t[:, n : n + w], preferred_element_type=F32)
            psend[t, :, :, n : n + w] = r[0:64].astype(BF16).reshape(2, 32, w)
            copies[s].start()
            acc[t, :, :, n : n + w] = r[64:128].reshape(2, 32, w)

    def to_x(t):
        copies = pair_copies(t)
        for s, (n, w) in enumerate(GROUPS):
            copies[s].wait_recv()
            v = acc[t, :, :, n : n + w] + precv[t, :, :, n : n + w].astype(F32)
            acc[t, :, :, n : n + w] = v
            xsend[t, :, :, n : n + w] = v.astype(BF16)
            for i in range(2):
                pl.when(leaves(t, i))(lambda s=s, i=i: x_copy(t, s, i).start())

    mine = lax.rem(x, 2)

    def x_sum(t, s):
        q = t // 2
        n, w = GROUPS[s]
        for j in range(3):
            rc(
                xrecv.at[q, j, :, pl.ds(n, w)], xrecv.at[q, j, :, pl.ds(n, w)],
                xss.at[t, s, 0], xsr.at[q, s, j], x_peer[j],
            ).wait_recv()
        v = acc[t, pl.ds(mine, 1), :, n : n + w].reshape(32, w)
        for j in range(3):
            v = v + xrecv[q, j, :, n : n + w].astype(F32)
        return v

    z_copies = [
        rc(zsend.at[:, pl.ds(n, w)], zrecv.at[:, pl.ds(n, w)], zss.at[s], zsr.at[s], far)
        for s, (n, w) in enumerate(GROUPS)
    ]

    def to_far(t):
        for s, (n, w) in enumerate(GROUPS):
            zsend[:, n : n + w] = x_sum(t, s).astype(BF16)
            z_copies[s].start()

    def keep(t, s):
        n, w = GROUPS[s]
        total[:, n : n + w] = x_sum(t, s)

    c_pair = rc(cblk.at[1 - core], cprecv, cps, cpr, mate)
    c_x = [rc(cblk.at[core, xs[j]], cxrecv.at[j], cxs.at[j], cxr.at[j], x_peer[j]) for j in range(3)]
    c_far = rc(czsend.at[1 - zh], czrecv, czs, czr, far)

    def rounded():
        return low[...].reshape(32, 128)[:, 0:RANK]

    def adapter_gradient():
        pl.when(jnp.logical_not(at_source))(lambda: low_z[0].wait_recv())
        for c in local[4:]:
            c.wait()
        part = 0.5 * dot_tn(rounded(), act_v[...])
        for r in range(16):
            start = r * SLICE
            base, off = start // 128 * 128, start % 128
            if off + SLICE <= 128:
                b = part[:, base : base + 128]
                b = pltpu.roll(b, (128 - off) % 128, 1) if off else b
            else:
                b = pltpu.roll(part[:, base : base + 256], 256 - off, 1)[:, 0:128]
            cblk[r % 2, r // 4, (r // 2) % 2] = b
        c_pair.start()

    def comp_x():
        c_pair.wait_recv()
        cblk[pl.ds(core, 1)] = cblk[pl.ds(core, 1)] + cprecv[...][None]
        for d in c_x:
            d.start()

    def comp_far():
        for d in c_x:
            d.wait_recv()
        v = cblk[pl.ds(core, 1), pl.ds(x, 1)].reshape(2, 16, 128)
        for j in range(3):
            v = v + cxrecv[j]
        czsend[...] = v
        c_far.start()

    multiply(0)
    pass_three(4)
    to_x(0)
    low_to_y()
    multiply(2)
    low_to_z()
    multiply(1)
    to_x(1)
    pl.when(inside[0])(lambda: to_far(0))
    to_x(2)
    multiply(3)
    adapter_gradient()
    to_x(3)
    comp_x()
    pl.when(inside[1])(lambda: to_far(1))
    comp_far()

    for s, (n, w) in enumerate(GROUPS):
        term = jnp.dot(rounded(), down_v[:, n : n + w], preferred_element_type=F32)
        for t in (2, 3):
            pl.when(inside[t])(lambda t=t, s=s: keep(t, s))
        total[:, n : n + w] += 0.5 * term

    for s, (n, w) in enumerate(GROUPS):
        z_copies[s].wait_recv()
        out[:, n : n + w] = (total[:, n : n + w] + zrecv[:, n : n + w].astype(F32)).astype(BF16)
    c_far.wait_recv()
    comp[...] = (czsend[pl.ds(zh, 1)].reshape(16, 128) + czrecv[...])[:, 0:SLICE]

    for d in sends:
        d.wait_send()
    for t in range(4):
        for d in pair_copies(t):
            d.wait_send()
        for i in range(2):

            def sent(t=t, i=i):
                for s in range(NG):
                    x_copy(t, s, i).wait_send()

            pl.when(leaves(t, i))(sent)
    for d in [low_mate, *low_x, low_far, c_pair, c_far, *c_x, *z_copies]:
        d.wait_send()
    for b in (0, 1):
        pl.when(is_source[b])(lambda b=b: [d.wait_send() for d in low_y[b]] and None)
    pl.when(at_source)(lambda: [d.wait_send() for d in low_z] and None)


def write_out(a, b, c, d, sems):
    copies = [pltpu.make_async_copy(a, c, sems.at[0]), pltpu.make_async_copy(b, d, sems.at[1])]
    for v in copies:
        v.start()
    for v in copies:
        v.wait()


def on_device(grad, codes, scale, down, up, act):
    hidden, width = codes.shape
    any_ = pl.BlockSpec(memory_space=pl.ANY)
    vmem = pl.BlockSpec(memory_space=pltpu.VMEM)
    dma = pltpu.SemaphoreType.DMA
    out, comp = pl.pallas_call(
        kernel,
        out_shape=(
            jax.ShapeDtypeStruct((32, hidden), BF16),
            jax.ShapeDtypeStruct((16, SLICE), F32),
        ),
        in_specs=[any_] * 6,
        out_specs=(vmem, vmem),
        scratch_shapes=[
            pltpu.VMEM((32, 16, width), BF16),
            pltpu.VMEM((hidden, width), BF16),
            pltpu.VMEM((width, hidden), BF16),
            pltpu.VMEM((1, width), F32),
            pltpu.VMEM((16, hidden), BF16),
            pltpu.VMEM((16, width), BF16),
            pltpu.VMEM((32, hidden), BF16),
            pltpu.VMEM((4, 128, width), BF16),
            pltpu.VMEM((4, 2, 32, hidden), F32),
            pltpu.VMEM((4, 2, 32, hidden), BF16),
            pltpu.VMEM((4, 2, 32, hidden), BF16),
            pltpu.VMEM((4, 2, 32, hidden), BF16),
            pltpu.VMEM((2, 3, 32, hidden), BF16),
            pltpu.VMEM((32, hidden), BF16),
            pltpu.VMEM((32, hidden), BF16),
            pltpu.VMEM((32, hidden), F32),
            pltpu.VMEM((3, 16, 128), F32),
            pltpu.VMEM((16, 128), F32),
            pltpu.VMEM((3, 16, 128), F32),
            pltpu.VMEM((16, 128), F32),
            pltpu.VMEM((2, 16, 128), BF16),
            pltpu.VMEM((2, 4, 2, 16, 128), F32),
            pltpu.VMEM((4, 2, 16, 128), F32),
            pltpu.VMEM((3, 2, 16, 128), F32),
            pltpu.VMEM((2, 16, 128), F32),
            pltpu.VMEM((16, 128), F32),
            pltpu.SemaphoreType.REGULAR,
            dma((6,)),
            dma((8,)), dma((8,)), dma((8, 3)), dma((8, 3)),
            dma((4, NG)), dma((4, NG)), dma((4, NG, 2)), dma((2, NG, 3)), dma((NG,)), dma((NG,)),
            dma, dma, dma((3,)), dma((3,)), dma, dma, dma((2, 3)), dma((2,)), dma((8,)), dma,
            dma, dma, dma((3,)), dma((3,)), dma, dma,
        ],
        compiler_params=pltpu.CompilerParams(
            collective_id=0, has_side_effects=True, vmem_limit_bytes=60 * 2**20
        ),
        cost_estimate=pl.CostEstimate(flops=2 * 512 * hidden * width, bytes_accessed=4 * 2**20, transcendentals=0),
    )(grad, codes, scale.reshape(1, width), down, up, act)
    return tuple(
        pl.pallas_call(
            write_out,
            out_shape=(
                jax.ShapeDtypeStruct((32, hidden), BF16),
                jax.ShapeDtypeStruct((16, SLICE), F32),
            ),
            in_specs=[vmem, vmem],
            out_specs=(any_, any_),
            scratch_shapes=[dma((2,))],
            compiler_params=pltpu.CompilerParams(has_side_effects=True),
        )(out, comp)
    )


def solution(mesh):
    return jax.shard_map(
        on_device,
        mesh=mesh,
        in_specs=(
            P("col", "row"),
            P("col", "row"),
            P("row"),
            P(None, "col"),
            P(None, "row"),
            P("row", "col"),
        ),
        out_specs=(P("row", "col"), P(None, ("col", "row"))),
        check_vma=False,
    )
```

```python
import jax
import jax.numpy as jnp
from jax import lax
from jax.experimental import pallas as pl
from jax.experimental.pallas import tpu as pltpu
from jax.sharding import PartitionSpec as P

MESH = pl.DeviceIdType.MESH
F32, BF16 = jnp.float32, jnp.bfloat16
GROUPS = ((0, 768), (768, 896))
NG = len(GROUPS)
SLICE = 104
RANK = 16


def flip(v, b):
    return v + b - 2 * b * lax.rem(lax.div(v, b), 2)


def dot_nt(a, b):
    return lax.dot_general(a, b, (((1,), (1,)), ((), ())), preferred_element_type=F32)


def dot_tn(a, b):
    return lax.dot_general(a, b, (((0,), (0,)), ((), ())), preferred_element_type=F32)


def kernel(
    grad, codes, scale, down, up, act, out, comp,
    gbuf, codes_v, codes_t, scale_v, down_v, up_v, act_v, lhs, acc, psend, precv, xsend, xrecv, zsend, zrecv, total,
    lsum, lmate, lx, lfar, low, cblk, cprecv, cxrecv, czsend, czrecv,
    far_in, lsem, gzs, gzr, gys, gyr, pss, psr, xss, xsr, zss, zsr,
    lps, lpr, lxs, lxr, lfs, lfr, lys, lyr, lzs, lzr, cps, cpr, cxs, cxr, czs, czr,
):
    row, col = lax.axis_index("row"), lax.axis_index("col")
    core, zh, x = lax.rem(row, 2), lax.rem(lax.div(row, 2), 2), lax.div(row, 4)
    y, zl = lax.rem(col, 4), lax.div(col, 4)

    def at_row(x_, zh_, core_):
        return {"row": x_ * 4 + zh_ * 2 + core_, "col": col}

    def at_col(zl_, y_):
        return {"row": row, "col": zl_ * 4 + y_}

    def zmap(m):
        v = zl
        for b in (1, 2, 4):
            if m & b:
                v = flip(v, b)
        return v

    mate = at_row(x, zh, 1 - core)
    far = at_row(x, 1 - zh, core)
    cross = {"row": x * 4 + (1 - zh) * 2 + core, "col": zmap(4) * 4 + y}
    xs = [lax.rem(x + j, 4) for j in (1, 2, 3)]
    x_peer = [at_row(v, zh, core) for v in xs]
    y_peer = [at_col(zl, lax.rem(y + j, 4)) for j in (1, 2, 3)]
    z_peer = {m: at_col(zmap(m), y) for m in (1, 2, 3, 4)}

    def rc(src, dst, ss, rs, dev):
        return pltpu.make_async_remote_copy(
            src_ref=src, dst_ref=dst, send_sem=ss, recv_sem=rs, device_id=dev, device_id_type=MESH
        )

    local = [
        pltpu.make_async_copy(s, d, lsem.at[i])
        for i, (s, d) in enumerate(
            ((grad, gbuf.at[col]), (scale, scale_v), (up, up_v), (codes, codes_v), (down, down_v), (act, act_v))
        )
    ]
    for c in local:
        c.start()

    barrier = pltpu.get_barrier_semaphore()
    peers = [z_peer[4], cross, z_peer[3], z_peer[2], z_peer[1], *x_peer, *y_peer, mate]
    for p in peers:
        pl.semaphore_signal(barrier, inc=1, device_id=p, device_id_type=MESH)
    local[0].wait()
    local[2].wait()
    lsum[...] = jnp.zeros_like(lsum)
    lsum[0, :, 0:RANK] = dot_nt(gbuf[pl.ds(col, 1)].reshape(16, -1), up_v[...])
    low_mate = rc(lsum.at[0], lmate, lps, lpr, mate)
    low_x = [rc(lsum.at[1], lx.at[j], lxs.at[j], lxr.at[j], x_peer[j]) for j in range(3)]
    low_far = rc(lsum.at[2], lfar, lfs, lfr, far)
    pl.semaphore_wait(barrier, len(peers))
    pl.semaphore_signal(far_in, inc=1, device_id=z_peer[4], device_id_type=MESH)

    sends = []

    def pass_on(m, bits):
        k = zmap(m)
        c = k * 4 + y
        for b in bits:
            d = rc(gbuf.at[c], gbuf.at[c], gzs.at[m ^ b], gzr.at[m ^ b], z_peer[b])
            d.start()
            sends.append(d)
        for j in range(3):
            d = rc(gbuf.at[c], gbuf.at[c], gys.at[k, j], gyr.at[k, j], y_peer[j])
            d.start()
            sends.append(d)

    def z_wait(m):
        c = zmap(m) * 4 + y
        rc(gbuf.at[c], gbuf.at[c], gzs.at[m], gzr.at[m], z_peer[1]).wait_recv()

    odd = 1 - lax.rem(zl + zh, 2)

    def pass_three(base):
        even_k, odd_k = [zmap(base + 2)], [zmap(base + 1), zmap(base + 3)]
        for m, k in (
            (base + 2 - odd, odd * odd_k[0] + (1 - odd) * even_k[0]),
            (base + 1 + 2 * odd, odd * odd_k[1] + (1 - odd) * odd_k[0]),
            (base + 3 - odd, odd * even_k[0] + (1 - odd) * odd_k[1]),
        ):
            c = k * 4 + y
            rc(gbuf.at[c], gbuf.at[c], gzs.at[m], gzr.at[m], z_peer[1]).wait_recv()
            for j in range(3):
                d = rc(gbuf.at[c], gbuf.at[c], gys.at[k, j], gyr.at[k, j], y_peer[j])
                d.start()
                sends.append(d)

    pass_on(0, (4, 2, 1, 3))
    low_mate.start()
    local[1].wait()
    local[3].wait()
    for n in range(0, codes_v.shape[0], 128):
        codes_t[:, n : n + 128] = codes_v[n : n + 128, :].T
    low_mate.wait_recv()
    lsum[1] = lsum[0] + lmate[...]
    for d in low_x:
        d.start()
    pass_three(0)
    lsum[2] = lsum[1]
    for j in range(3):
        low_x[j].wait_recv()
        lsum[2] += lx[j]
    pl.semaphore_wait(far_in, 1)
    low_far.start()
    z_wait(4)
    pass_on(4, (3, 2, 1))

    at_source = zl == 2 * x + zh
    is_source = [at_source & (lax.div(y, 2) == core) & (lax.rem(y, 2) == b) for b in (0, 1)]
    low_y = [[rc(low.at[b], low.at[b], lys.at[b, j], lyr.at[b], y_peer[j]) for j in range(3)] for b in (0, 1)]
    low_z = [rc(low, low, lzs.at[m], lzr, at_col(zmap(m), y)) for m in range(1, 8)]

    def low_to_y():
        low_far.wait_recv()
        whole = (lsum[2] + lfar[...]).astype(BF16)
        for b in (0, 1):

            def give(b=b):
                low[b] = whole
                for d in low_y[b]:
                    d.start()

            pl.when(is_source[b])(give)

    def low_to_z():
        for b in (0, 1):
            pl.when(at_source & jnp.logical_not(is_source[b]))(lambda b=b: low_y[b][0].wait_recv())

        def give():
            for d in low_z:
                d.start()

        pl.when(at_source)(give)

    half = lax.div(zl, 4)
    half_of = [half, 1 - half, half, 1 - half]
    parity_of = [1 - zh, 1 - zh, zh, zh]
    inside = [lax.div(x, 2) == h for h in half_of]

    def pair_copies(t):
        return [
            rc(psend.at[t, :, :, pl.ds(n, w)], precv.at[t, :, :, pl.ds(n, w)], pss.at[t, s], psr.at[t, s], mate)
            for s, (n, w) in enumerate(GROUPS)
        ]

    def x_copy(t, s, i):
        n, w = GROUPS[s]
        d = 2 * half_of[t] + i
        j = lax.rem(d - x + 3, 4)
        return rc(
            xsend.at[t, i, :, pl.ds(n, w)], xrecv.at[t // 2, j, :, pl.ds(n, w)],
            xss.at[t, s, i], xsr.at[t // 2, s, j], at_row(d, zh, core),
        )

    def leaves(t, i):
        return x != 2 * half_of[t] + i

    def multiply(t):
        for v in range(2):
            k = 4 * half_of[t] + 2 * v + parity_of[t]
            for j in range(3):
                c = k * 4 + lax.rem(y + 3 - j, 4)
                rc(gbuf.at[c], gbuf.at[c], gys.at[k, j], gyr.at[k, j], y_peer[j]).wait_recv()
        for i, c_ in enumerate((1 - core, core)):
            for v in range(2):
                k = 4 * half_of[t] + 2 * v + parity_of[t]
                g = gbuf[pl.ds(k * 4 + 2 * c_, 2)].reshape(32, 1024)
                n = i * 64 + v * 32
                lhs[t, n : n + 32, :] = (g.astype(F32) * scale_v[...]).astype(BF16)
        copies = pair_copies(t)
        for s, (n, w) in enumerate(GROUPS):
            r = jnp.dot(lhs[t], codes_t[:, n : n + w], preferred_element_type=F32)
            psend[t, :, :, n : n + w] = r[0:64].astype(BF16).reshape(2, 32, w)
            copies[s].start()
            acc[t, :, :, n : n + w] = r[64:128].reshape(2, 32, w)

    def to_x(t):
        copies = pair_copies(t)
        for s, (n, w) in enumerate(GROUPS):
            copies[s].wait_recv()
            v = acc[t, :, :, n : n + w] + precv[t, :, :, n : n + w].astype(F32)
            acc[t, :, :, n : n + w] = v
            xsend[t, :, :, n : n + w] = v.astype(BF16)
            for i in range(2):
                pl.when(leaves(t, i))(lambda s=s, i=i: x_copy(t, s, i).start())

    mine = lax.rem(x, 2)

    def x_sum(t, s):
        q = t // 2
        n, w = GROUPS[s]
        for j in range(3):
            rc(
                xrecv.at[q, j, :, pl.ds(n, w)], xrecv.at[q, j, :, pl.ds(n, w)],
                xss.at[t, s, 0], xsr.at[q, s, j], x_peer[j],
            ).wait_recv()
        v = acc[t, pl.ds(mine, 1), :, n : n + w].reshape(32, w)
        for j in range(3):
            v = v + xrecv[q, j, :, n : n + w].astype(F32)
        return v

    z_copies = [
        rc(zsend.at[:, pl.ds(n, w)], zrecv.at[:, pl.ds(n, w)], zss.at[s], zsr.at[s], far)
        for s, (n, w) in enumerate(GROUPS)
    ]

    def to_far(t):
        for s, (n, w) in enumerate(GROUPS):
            zsend[:, n : n + w] = x_sum(t, s).astype(BF16)
            z_copies[s].start()

    def keep(t, s):
        n, w = GROUPS[s]
        total[:, n : n + w] = x_sum(t, s)

    c_pair = rc(cblk.at[1 - core], cprecv, cps, cpr, mate)
    c_x = [rc(cblk.at[core, xs[j]], cxrecv.at[j], cxs.at[j], cxr.at[j], x_peer[j]) for j in range(3)]
    c_far = rc(czsend.at[1 - zh], czrecv, czs, czr, far)

    def rounded():
        return low[...].reshape(32, 128)[:, 0:RANK]

    def adapter_gradient():
        pl.when(jnp.logical_not(at_source))(lambda: low_z[0].wait_recv())
        for c in local[4:]:
            c.wait()
        part = 0.5 * dot_tn(rounded(), act_v[...])
        for r in range(16):
            start = r * SLICE
            base, off = start // 128 * 128, start % 128
            if off + SLICE <= 128:
                b = part[:, base : base + 128]
                b = pltpu.roll(b, (128 - off) % 128, 1) if off else b
            else:
                b = pltpu.roll(part[:, base : base + 256], 256 - off, 1)[:, 0:128]
            cblk[r % 2, r // 4, (r // 2) % 2] = b
        c_pair.start()

    def comp_x():
        c_pair.wait_recv()
        cblk[pl.ds(core, 1)] = cblk[pl.ds(core, 1)] + cprecv[...][None]
        for d in c_x:
            d.start()

    def comp_far():
        for d in c_x:
            d.wait_recv()
        v = cblk[pl.ds(core, 1), pl.ds(x, 1)].reshape(2, 16, 128)
        for j in range(3):
            v = v + cxrecv[j]
        czsend[...] = v
        c_far.start()

    multiply(0)
    pass_three(4)
    to_x(0)
    low_to_y()
    multiply(2)
    low_to_z()
    multiply(1)
    to_x(1)
    pl.when(inside[0])(lambda: to_far(0))
    to_x(2)
    multiply(3)
    adapter_gradient()
    to_x(3)
    comp_x()
    pl.when(inside[1])(lambda: to_far(1))
    comp_far()

    for s, (n, w) in enumerate(GROUPS):
        term = jnp.dot(rounded(), down_v[:, n : n + w], preferred_element_type=F32)
        for t in (2, 3):
            pl.when(inside[t])(lambda t=t, s=s: keep(t, s))
        total[:, n : n + w] += 0.5 * term

    for s, (n, w) in enumerate(GROUPS):
        z_copies[s].wait_recv()
        out[:, n : n + w] = (total[:, n : n + w] + zrecv[:, n : n + w].astype(F32)).astype(BF16)
    c_far.wait_recv()
    comp[...] = (czsend[pl.ds(zh, 1)].reshape(16, 128) + czrecv[...])[:, 0:SLICE]

    for d in sends:
        d.wait_send()
    for t in range(4):
        for d in pair_copies(t):
            d.wait_send()
        for i in range(2):

            def sent(t=t, i=i):
                for s in range(NG):
                    x_copy(t, s, i).wait_send()

            pl.when(leaves(t, i))(sent)
    for d in [low_mate, *low_x, low_far, c_pair, c_far, *c_x, *z_copies]:
        d.wait_send()
    for b in (0, 1):
        pl.when(is_source[b])(lambda b=b: [d.wait_send() for d in low_y[b]] and None)
    pl.when(at_source)(lambda: [d.wait_send() for d in low_z] and None)


def write_out(a, b, c, d, sems):
    copies = [pltpu.make_async_copy(a, c, sems.at[0]), pltpu.make_async_copy(b, d, sems.at[1])]
    for v in copies:
        v.start()
    for v in copies:
        v.wait()


def on_device(grad, codes, scale, down, up, act):
    hidden, width = codes.shape
    any_ = pl.BlockSpec(memory_space=pl.ANY)
    vmem = pl.BlockSpec(memory_space=pltpu.VMEM)
    dma = pltpu.SemaphoreType.DMA
    out, comp = pl.pallas_call(
        kernel,
        out_shape=(
            jax.ShapeDtypeStruct((32, hidden), BF16),
            jax.ShapeDtypeStruct((16, SLICE), F32),
        ),
        in_specs=[any_] * 6,
        out_specs=(vmem, vmem),
        scratch_shapes=[
            pltpu.VMEM((32, 16, width), BF16),
            pltpu.VMEM((hidden, width), BF16),
            pltpu.VMEM((width, hidden), BF16),
            pltpu.VMEM((1, width), F32),
            pltpu.VMEM((16, hidden), BF16),
            pltpu.VMEM((16, width), BF16),
            pltpu.VMEM((32, hidden), BF16),
            pltpu.VMEM((4, 128, width), BF16),
            pltpu.VMEM((4, 2, 32, hidden), F32),
            pltpu.VMEM((4, 2, 32, hidden), BF16),
            pltpu.VMEM((4, 2, 32, hidden), BF16),
            pltpu.VMEM((4, 2, 32, hidden), BF16),
            pltpu.VMEM((2, 3, 32, hidden), BF16),
            pltpu.VMEM((32, hidden), BF16),
            pltpu.VMEM((32, hidden), BF16),
            pltpu.VMEM((32, hidden), F32),
            pltpu.VMEM((3, 16, 128), F32),
            pltpu.VMEM((16, 128), F32),
            pltpu.VMEM((3, 16, 128), F32),
            pltpu.VMEM((16, 128), F32),
            pltpu.VMEM((2, 16, 128), BF16),
            pltpu.VMEM((2, 4, 2, 16, 128), F32),
            pltpu.VMEM((4, 2, 16, 128), F32),
            pltpu.VMEM((3, 2, 16, 128), F32),
            pltpu.VMEM((2, 16, 128), F32),
            pltpu.VMEM((16, 128), F32),
            pltpu.SemaphoreType.REGULAR,
            dma((6,)),
            dma((8,)), dma((8,)), dma((8, 3)), dma((8, 3)),
            dma((4, NG)), dma((4, NG)), dma((4, NG, 2)), dma((2, NG, 3)), dma((NG,)), dma((NG,)),
            dma, dma, dma((3,)), dma((3,)), dma, dma, dma((2, 3)), dma((2,)), dma((8,)), dma,
            dma, dma, dma((3,)), dma((3,)), dma, dma,
        ],
        compiler_params=pltpu.CompilerParams(
            collective_id=0, has_side_effects=True, vmem_limit_bytes=60 * 2**20
        ),
        cost_estimate=pl.CostEstimate(flops=2 * 512 * hidden * width, bytes_accessed=4 * 2**20, transcendentals=0),
    )(grad, codes, scale.reshape(1, width), down, up, act)
    return tuple(
        pl.pallas_call(
            write_out,
            out_shape=(
                jax.ShapeDtypeStruct((32, hidden), BF16),
                jax.ShapeDtypeStruct((16, SLICE), F32),
            ),
            in_specs=[vmem, vmem],
            out_specs=(any_, any_),
            scratch_shapes=[dma((2,))],
            compiler_params=pltpu.CompilerParams(has_side_effects=True),
        )(out, comp)
    )


def solution(mesh):
    return jax.shard_map(
        on_device,
        mesh=mesh,
        in_specs=(
            P("col", "row"),
            P("col", "row"),
            P("row"),
            P(None, "col"),
            P(None, "row"),
            P("row", "col"),
        ),
        out_specs=(P("row", "col"), P(None, ("col", "row"))),
        check_vma=False,
    )
```

```python
import jax
import jax.numpy as jnp
from jax import lax
from jax.experimental import pallas as pl
from jax.experimental.pallas import tpu as pltpu
from jax.sharding import PartitionSpec as P

MESH = pl.DeviceIdType.MESH
F32, BF16 = jnp.float32, jnp.bfloat16
GROUPS = ((0, 1024), (1024, 640))
NG = len(GROUPS)
SLICE = 104
RANK = 16


def flip(v, b):
    return v + b - 2 * b * lax.rem(lax.div(v, b), 2)


def dot_nt(a, b):
    return lax.dot_general(a, b, (((1,), (1,)), ((), ())), preferred_element_type=F32)


def dot_tn(a, b):
    return lax.dot_general(a, b, (((0,), (0,)), ((), ())), preferred_element_type=F32)


def kernel(
    grad, codes, scale, down, up, act, out, comp,
    gbuf, codes_v, codes_t, scale_v, down_v, up_v, act_v, lhs, acc, psend, precv, xsend, xrecv, zsend, zrecv, total,
    lsum, lmate, lx, lfar, low, cblk, cprecv, cxrecv, czsend, czrecv,
    far_in, lsem, gzs, gzr, gys, gyr, pss, psr, xss, xsr, zss, zsr,
    lps, lpr, lxs, lxr, lfs, lfr, lys, lyr, lzs, lzr, cps, cpr, cxs, cxr, czs, czr,
):
    row, col = lax.axis_index("row"), lax.axis_index("col")
    core, zh, x = lax.rem(row, 2), lax.rem(lax.div(row, 2), 2), lax.div(row, 4)
    y, zl = lax.rem(col, 4), lax.div(col, 4)

    def at_row(x_, zh_, core_):
        return {"row": x_ * 4 + zh_ * 2 + core_, "col": col}

    def at_col(zl_, y_):
        return {"row": row, "col": zl_ * 4 + y_}

    def zmap(m):
        v = zl
        for b in (1, 2, 4):
            if m & b:
                v = flip(v, b)
        return v

    mate = at_row(x, zh, 1 - core)
    far = at_row(x, 1 - zh, core)
    cross = {"row": x * 4 + (1 - zh) * 2 + core, "col": zmap(4) * 4 + y}
    xs = [lax.rem(x + j, 4) for j in (1, 2, 3)]
    x_peer = [at_row(v, zh, core) for v in xs]
    y_peer = [at_col(zl, lax.rem(y + j, 4)) for j in (1, 2, 3)]
    z_peer = {m: at_col(zmap(m), y) for m in (1, 2, 3, 4)}

    def rc(src, dst, ss, rs, dev):
        return pltpu.make_async_remote_copy(
            src_ref=src, dst_ref=dst, send_sem=ss, recv_sem=rs, device_id=dev, device_id_type=MESH
        )

    local = [
        pltpu.make_async_copy(s, d, lsem.at[i])
        for i, (s, d) in enumerate(
            ((grad, gbuf.at[col]), (scale, scale_v), (up, up_v), (codes, codes_v), (down, down_v), (act, act_v))
        )
    ]
    for c in local:
        c.start()

    barrier = pltpu.get_barrier_semaphore()
    peers = [z_peer[4], cross, z_peer[3], z_peer[2], z_peer[1], *x_peer, *y_peer, mate]
    for p in peers:
        pl.semaphore_signal(barrier, inc=1, device_id=p, device_id_type=MESH)
    local[0].wait()
    local[2].wait()
    lsum[...] = jnp.zeros_like(lsum)
    lsum[0, :, 0:RANK] = dot_nt(gbuf[pl.ds(col, 1)].reshape(16, -1), up_v[...])
    low_mate = rc(lsum.at[0], lmate, lps, lpr, mate)
    low_x = [rc(lsum.at[1], lx.at[j], lxs.at[j], lxr.at[j], x_peer[j]) for j in range(3)]
    low_far = rc(lsum.at[2], lfar, lfs, lfr, far)
    pl.semaphore_wait(barrier, len(peers))
    pl.semaphore_signal(far_in, inc=1, device_id=z_peer[4], device_id_type=MESH)

    sends = []

    def pass_on(m, bits):
        k = zmap(m)
        c = k * 4 + y
        for b in bits:
            d = rc(gbuf.at[c], gbuf.at[c], gzs.at[m ^ b], gzr.at[m ^ b], z_peer[b])
            d.start()
            sends.append(d)
        for j in range(3):
            d = rc(gbuf.at[c], gbuf.at[c], gys.at[k, j], gyr.at[k, j], y_peer[j])
            d.start()
            sends.append(d)

    def z_wait(m):
        c = zmap(m) * 4 + y
        rc(gbuf.at[c], gbuf.at[c], gzs.at[m], gzr.at[m], z_peer[1]).wait_recv()

    odd = 1 - lax.rem(zl + zh, 2)

    def pass_three(base):
        even_k, odd_k = [zmap(base + 2)], [zmap(base + 1), zmap(base + 3)]
        for m, k in (
            (base + 2 - odd, odd * odd_k[0] + (1 - odd) * even_k[0]),
            (base + 1 + 2 * odd, odd * odd_k[1] + (1 - odd) * odd_k[0]),
            (base + 3 - odd, odd * even_k[0] + (1 - odd) * odd_k[1]),
        ):
            c = k * 4 + y
            rc(gbuf.at[c], gbuf.at[c], gzs.at[m], gzr.at[m], z_peer[1]).wait_recv()
            for j in range(3):
                d = rc(gbuf.at[c], gbuf.at[c], gys.at[k, j], gyr.at[k, j], y_peer[j])
                d.start()
                sends.append(d)

    pass_on(0, (4, 2, 1, 3))
    low_mate.start()
    local[1].wait()
    local[3].wait()
    for n in range(0, codes_v.shape[0], 128):
        codes_t[:, n : n + 128] = codes_v[n : n + 128, :].T
    low_mate.wait_recv()
    lsum[1] = lsum[0] + lmate[...]
    for d in low_x:
        d.start()
    pass_three(0)
    lsum[2] = lsum[1]
    for j in range(3):
        low_x[j].wait_recv()
        lsum[2] += lx[j]
    pl.semaphore_wait(far_in, 1)
    low_far.start()
    z_wait(4)
    pass_on(4, (3, 2, 1))

    at_source = zl == 2 * x + zh
    is_source = [at_source & (lax.div(y, 2) == core) & (lax.rem(y, 2) == b) for b in (0, 1)]
    low_y = [[rc(low.at[b], low.at[b], lys.at[b, j], lyr.at[b], y_peer[j]) for j in range(3)] for b in (0, 1)]
    low_z = [rc(low, low, lzs.at[m], lzr, at_col(zmap(m), y)) for m in range(1, 8)]

    def low_to_y():
        low_far.wait_recv()
        whole = (lsum[2] + lfar[...]).astype(BF16)
        for b in (0, 1):

            def give(b=b):
                low[b] = whole
                for d in low_y[b]:
                    d.start()

            pl.when(is_source[b])(give)

    def low_to_z():
        for b in (0, 1):
            pl.when(at_source & jnp.logical_not(is_source[b]))(lambda b=b: low_y[b][0].wait_recv())

        def give():
            for d in low_z:
                d.start()

        pl.when(at_source)(give)

    half = lax.div(zl, 4)
    half_of = [half, 1 - half, half, 1 - half]
    parity_of = [1 - zh, 1 - zh, zh, zh]
    inside = [lax.div(x, 2) == h for h in half_of]

    def pair_copies(t):
        return [
            rc(psend.at[t, :, :, pl.ds(n, w)], precv.at[t, :, :, pl.ds(n, w)], pss.at[t, s], psr.at[t, s], mate)
            for s, (n, w) in enumerate(GROUPS)
        ]

    def x_copy(t, s, i):
        n, w = GROUPS[s]
        d = 2 * half_of[t] + i
        j = lax.rem(d - x + 3, 4)
        return rc(
            xsend.at[t, i, :, pl.ds(n, w)], xrecv.at[t // 2, j, :, pl.ds(n, w)],
            xss.at[t, s, i], xsr.at[t // 2, s, j], at_row(d, zh, core),
        )

    def leaves(t, i):
        return x != 2 * half_of[t] + i

    def multiply(t):
        for v in range(2):
            k = 4 * half_of[t] + 2 * v + parity_of[t]
            for j in range(3):
                c = k * 4 + lax.rem(y + 3 - j, 4)
                rc(gbuf.at[c], gbuf.at[c], gys.at[k, j], gyr.at[k, j], y_peer[j]).wait_recv()
        for i, c_ in enumerate((1 - core, core)):
            for v in range(2):
                k = 4 * half_of[t] + 2 * v + parity_of[t]
                g = gbuf[pl.ds(k * 4 + 2 * c_, 2)].reshape(32, 1024)
                n = i * 64 + v * 32
                lhs[t, n : n + 32, :] = (g.astype(F32) * scale_v[...]).astype(BF16)
        copies = pair_copies(t)
        for s, (n, w) in enumerate(GROUPS):
            r = jnp.dot(lhs[t], codes_t[:, n : n + w], preferred_element_type=F32)
            psend[t, :, :, n : n + w] = r[0:64].astype(BF16).reshape(2, 32, w)
            copies[s].start()
            acc[t, :, :, n : n + w] = r[64:128].reshape(2, 32, w)

    def to_x(t):
        copies = pair_copies(t)
        for s, (n, w) in enumerate(GROUPS):
            copies[s].wait_recv()
            v = acc[t, :, :, n : n + w] + precv[t, :, :, n : n + w].astype(F32)
            acc[t, :, :, n : n + w] = v
            xsend[t, :, :, n : n + w] = v.astype(BF16)
            for i in range(2):
                pl.when(leaves(t, i))(lambda s=s, i=i: x_copy(t, s, i).start())

    mine = lax.rem(x, 2)

    def x_sum(t, s):
        q = t // 2
        n, w = GROUPS[s]
        for j in range(3):
            rc(
                xrecv.at[q, j, :, pl.ds(n, w)], xrecv.at[q, j, :, pl.ds(n, w)],
                xss.at[t, s, 0], xsr.at[q, s, j], x_peer[j],
            ).wait_recv()
        v = acc[t, pl.ds(mine, 1), :, n : n + w].reshape(32, w)
        for j in range(3):
            v = v + xrecv[q, j, :, n : n + w].astype(F32)
        return v

    z_copies = [
        rc(zsend.at[:, pl.ds(n, w)], zrecv.at[:, pl.ds(n, w)], zss.at[s], zsr.at[s], far)
        for s, (n, w) in enumerate(GROUPS)
    ]

    def to_far(t):
        for s, (n, w) in enumerate(GROUPS):
            zsend[:, n : n + w] = x_sum(t, s).astype(BF16)
            z_copies[s].start()

    def keep(t, s):
        n, w = GROUPS[s]
        total[:, n : n + w] = x_sum(t, s)

    c_pair = rc(cblk.at[1 - core], cprecv, cps, cpr, mate)
    c_x = [rc(cblk.at[core, xs[j]], cxrecv.at[j], cxs.at[j], cxr.at[j], x_peer[j]) for j in range(3)]
    c_far = rc(czsend.at[1 - zh], czrecv, czs, czr, far)

    def rounded():
        return low[...].reshape(32, 128)[:, 0:RANK]

    def adapter_gradient():
        pl.when(jnp.logical_not(at_source))(lambda: low_z[0].wait_recv())
        for c in local[4:]:
            c.wait()
        part = 0.5 * dot_tn(rounded(), act_v[...])
        for r in range(16):
            start = r * SLICE
            base, off = start // 128 * 128, start % 128
            if off + SLICE <= 128:
                b = part[:, base : base + 128]
                b = pltpu.roll(b, (128 - off) % 128, 1) if off else b
            else:
                b = pltpu.roll(part[:, base : base + 256], 256 - off, 1)[:, 0:128]
            cblk[r % 2, r // 4, (r // 2) % 2] = b
        c_pair.start()

    def comp_x():
        c_pair.wait_recv()
        cblk[pl.ds(core, 1)] = cblk[pl.ds(core, 1)] + cprecv[...][None]
        for d in c_x:
            d.start()

    def comp_far():
        for d in c_x:
            d.wait_recv()
        v = cblk[pl.ds(core, 1), pl.ds(x, 1)].reshape(2, 16, 128)
        for j in range(3):
            v = v + cxrecv[j]
        czsend[...] = v
        c_far.start()

    multiply(0)
    pass_three(4)
    to_x(0)
    low_to_y()
    multiply(2)
    low_to_z()
    multiply(1)
    to_x(1)
    pl.when(inside[0])(lambda: to_far(0))
    to_x(2)
    multiply(3)
    adapter_gradient()
    to_x(3)
    comp_x()
    pl.when(inside[1])(lambda: to_far(1))
    comp_far()

    for s, (n, w) in enumerate(GROUPS):
        term = jnp.dot(rounded(), down_v[:, n : n + w], preferred_element_type=F32)
        for t in (2, 3):
            pl.when(inside[t])(lambda t=t, s=s: keep(t, s))
        total[:, n : n + w] += 0.5 * term

    for s, (n, w) in enumerate(GROUPS):
        z_copies[s].wait_recv()
        out[:, n : n + w] = (total[:, n : n + w] + zrecv[:, n : n + w].astype(F32)).astype(BF16)
    c_far.wait_recv()
    comp[...] = (czsend[pl.ds(zh, 1)].reshape(16, 128) + czrecv[...])[:, 0:SLICE]

    for d in sends:
        d.wait_send()
    for t in range(4):
        for d in pair_copies(t):
            d.wait_send()
        for i in range(2):

            def sent(t=t, i=i):
                for s in range(NG):
                    x_copy(t, s, i).wait_send()

            pl.when(leaves(t, i))(sent)
    for d in [low_mate, *low_x, low_far, c_pair, c_far, *c_x, *z_copies]:
        d.wait_send()
    for b in (0, 1):
        pl.when(is_source[b])(lambda b=b: [d.wait_send() for d in low_y[b]] and None)
    pl.when(at_source)(lambda: [d.wait_send() for d in low_z] and None)


def write_out(a, b, c, d, sems):
    copies = [pltpu.make_async_copy(a, c, sems.at[0]), pltpu.make_async_copy(b, d, sems.at[1])]
    for v in copies:
        v.start()
    for v in copies:
        v.wait()


def on_device(grad, codes, scale, down, up, act):
    hidden, width = codes.shape
    any_ = pl.BlockSpec(memory_space=pl.ANY)
    vmem = pl.BlockSpec(memory_space=pltpu.VMEM)
    dma = pltpu.SemaphoreType.DMA
    out, comp = pl.pallas_call(
        kernel,
        out_shape=(
            jax.ShapeDtypeStruct((32, hidden), BF16),
            jax.ShapeDtypeStruct((16, SLICE), F32),
        ),
        in_specs=[any_] * 6,
        out_specs=(vmem, vmem),
        scratch_shapes=[
            pltpu.VMEM((32, 16, width), BF16),
            pltpu.VMEM((hidden, width), BF16),
            pltpu.VMEM((width, hidden), BF16),
            pltpu.VMEM((1, width), F32),
            pltpu.VMEM((16, hidden), BF16),
            pltpu.VMEM((16, width), BF16),
            pltpu.VMEM((32, hidden), BF16),
            pltpu.VMEM((4, 128, width), BF16),
            pltpu.VMEM((4, 2, 32, hidden), F32),
            pltpu.VMEM((4, 2, 32, hidden), BF16),
            pltpu.VMEM((4, 2, 32, hidden), BF16),
            pltpu.VMEM((4, 2, 32, hidden), BF16),
            pltpu.VMEM((2, 3, 32, hidden), BF16),
            pltpu.VMEM((32, hidden), BF16),
            pltpu.VMEM((32, hidden), BF16),
            pltpu.VMEM((32, hidden), F32),
            pltpu.VMEM((3, 16, 128), F32),
            pltpu.VMEM((16, 128), F32),
            pltpu.VMEM((3, 16, 128), F32),
            pltpu.VMEM((16, 128), F32),
            pltpu.VMEM((2, 16, 128), BF16),
            pltpu.VMEM((2, 4, 2, 16, 128), F32),
            pltpu.VMEM((4, 2, 16, 128), F32),
            pltpu.VMEM((3, 2, 16, 128), F32),
            pltpu.VMEM((2, 16, 128), F32),
            pltpu.VMEM((16, 128), F32),
            pltpu.SemaphoreType.REGULAR,
            dma((6,)),
            dma((8,)), dma((8,)), dma((8, 3)), dma((8, 3)),
            dma((4, NG)), dma((4, NG)), dma((4, NG, 2)), dma((2, NG, 3)), dma((NG,)), dma((NG,)),
            dma, dma, dma((3,)), dma((3,)), dma, dma, dma((2, 3)), dma((2,)), dma((8,)), dma,
            dma, dma, dma((3,)), dma((3,)), dma, dma,
        ],
        compiler_params=pltpu.CompilerParams(
            collective_id=0, has_side_effects=True, vmem_limit_bytes=60 * 2**20
        ),
        cost_estimate=pl.CostEstimate(flops=2 * 512 * hidden * width, bytes_accessed=4 * 2**20, transcendentals=0),
    )(grad, codes, scale.reshape(1, width), down, up, act)
    return tuple(
        pl.pallas_call(
            write_out,
            out_shape=(
                jax.ShapeDtypeStruct((32, hidden), BF16),
                jax.ShapeDtypeStruct((16, SLICE), F32),
            ),
            in_specs=[vmem, vmem],
            out_specs=(any_, any_),
            scratch_shapes=[dma((2,))],
            compiler_params=pltpu.CompilerParams(has_side_effects=True),
        )(out, comp)
    )


def solution(mesh):
    return jax.shard_map(
        on_device,
        mesh=mesh,
        in_specs=(
            P("col", "row"),
            P("col", "row"),
            P("row"),
            P(None, "col"),
            P(None, "row"),
            P("row", "col"),
        ),
        out_specs=(P("row", "col"), P(None, ("col", "row"))),
        check_vma=False,
    )
```
